32 devices in a mesh: groups: 2 (over x), ep: 4 (over z), et: 4 (over y, core).
Axes of the slice: x: 2, y: 2, z: 4, core: 2. Of those that a mesh axis runs over, the one named last changes fastest.
Arguments:
- hidden: bfloat16 [8, 768, 8192], P(('groups', 'ep'), None, 'et'), parts along dimension 0, may hold values from -1.75 to 1.75
- w_down: bfloat16 [4, 8192, 4096], P('ep', 'et'), may hold values from -0.09375 to 0.09375
- upstream: bfloat16 [2048, 4096], P(('groups', 'ep'), 'et'), parts along dimension 0, may hold values from -6 to 6
- expert_ids: int32 [2048, 2], P(('groups', 'ep')), parts along dimension 0, may hold values from 0 to 3, as said below
- combine: float32 [2048, 2], P(('groups', 'ep')), parts along dimension 0, may hold values from 0.09 to 1
Outputs:
- mixed: bfloat16 [2048, 4096], P(('groups', 'ep'), 'et'), parts along dimension 0
- grad_hidden: bfloat16 [8, 768, 8192], P(('groups', 'ep'), None, 'et'), parts along dimension 0
- grad_weight: bfloat16 [8, 8192, 4096], P(('groups', 'ep'), 'et'), parts along dimension 0
- balance: float32 [2], P('groups'), parts along dimension 0
The draws below stay inside these ranges and needn't reach their ends.
There are 2 independent parts, one for each index of `groups`. The reference program is written for one: setup_inputs(seed, part) draws one part's arguments, and reference() takes and returns one part's arrays. A program takes and returns all parts, laid end to end along the dimension named above; an argument that names none is the same for every part. Nothing has to cross between parts.
Inputs may be any that keep to these rules, and one draw needn't show every extreme that they name: `expert_ids`: each token names 2 different experts; among the 256 tokens of one index of ep no expert is named more than 192 times, and some expert exactly 192 times; every expert is named by some token.
All inputs are finite; a program needn't handle non-finite values.
Results may differ from the reference program's by a relative error of at most 0.01.
Values may be sent and summed in bfloat16 or wider, within the bound.
A program may use at most 192 MiB of HBM per device.

```python
import jax
import jax.numpy as jnp
import numpy as np
from jax import lax

D = 4096
FF = 8192
TOP = 2
TOK_DEV = 256
EXPERTS = 4
CAP = 192
ROWS = 768
TOKENS = 1024
N_EP = 4
N_ET = 4


def fill_table():
    remaining = TOP * TOK_DEV
    loads = []
    for expert in range(EXPERTS):
        taken = min(CAP, remaining)
        loads.append(taken)
        remaining = remaining - taken
    listed = np.repeat(np.arange(EXPERTS), loads).astype(np.int32)
    return jnp.asarray(listed).reshape(TOP, TOK_DEV).T


def draw_expert_ids(key, part):
    key = jax.random.fold_in(key, 11)
    key_shift, key_perm, key_flip = jax.random.split(key, 3)
    blocks = TOKENS // TOK_DEV
    base_rows = fill_table()
    shift = jax.random.randint(key_shift, (), 0, EXPERTS, dtype=jnp.int32)
    offsets = (jnp.arange(blocks, dtype=jnp.int32) + shift) % EXPERTS
    perm_keys = jax.random.split(key_perm, blocks)
    orders = jax.vmap(lambda one: jax.random.permutation(one, TOK_DEV))(perm_keys)
    rows = base_rows[orders]
    chosen = (rows + offsets[:, None, None]) % EXPERTS
    flips = jax.random.randint(key_flip, (blocks, TOK_DEV, 1), 0, 2, dtype=jnp.int32)
    chosen = jnp.where(flips == 1, chosen[:, :, ::-1], chosen)
    return chosen.reshape(TOKENS, TOP).astype(jnp.int32)


def draw_combine(key, part):
    key = jax.random.fold_in(key, 23)
    blocks = TOKENS // TOK_DEV
    position = (jnp.arange(TOKENS, dtype=jnp.int32) // TOK_DEV).astype(jnp.float32) / (blocks - 1)
    values = jax.random.uniform(key, (TOKENS, TOP), jnp.float32, 0.3, 1.0)
    factor = 0.33 + 0.67 * position
    return (values * factor[:, None]).astype(jnp.float32)


def with_spikes(drawn, rng, source, target, shards_of, factor):
    def block_of(dim):
        return (jnp.arange(drawn.shape[dim]) // (drawn.shape[dim] // shards_of)).reshape((-1,) + (1,) * (drawn.ndim - 1 - dim))

    one_side = jax.random.permutation(rng, shards_of)[block_of(target)]
    second = (block_of(target) + shards_of // 2) % shards_of
    return jnp.where((block_of(source) == one_side) | (block_of(source) == second), factor * drawn, drawn)


def shard_levels(key, shape, cuts, smallest, top_value):
    def one(axis_at, blocks):
        draws = jax.random.uniform(jax.random.fold_in(jax.random.fold_in(key, 6), axis_at), (blocks,), jnp.float32, smallest / len(cuts), top_value / len(cuts))
        return jnp.repeat(jnp.exp(draws), shape[axis_at] // blocks).reshape((-1,) + (1,) * (len(shape) - axis_at - 1))

    gain = one(*cuts[0])
    for cut in cuts[1:]:
        gain = gain * one(*cut)
    return gain


def bell_draw(stream_key, shape, scale, reach, cuts=(), held_as=jnp.bfloat16):
    level = shard_levels(stream_key, shape, cuts, -0.22, 0.18) if cuts else 1.0
    drawn = jax.random.normal(stream_key, shape, jnp.float32) * scale * level
    return jnp.minimum(jnp.maximum(drawn, -reach), reach).astype(held_as)


def heavy_noise(key, shape, width, bound, shards, heavy, kind=jnp.bfloat16):
    entries = width * jax.random.normal(key, shape, jnp.float32)
    if shards:
        entries = entries * shard_levels(key, shape, shards, -0.22, 0.18)
    return jnp.clip(with_spikes(entries, jax.random.fold_in(key, 3), *heavy), -bound, bound).astype(kind)


def setup_inputs(seed: int = 0, part: int = 0) -> dict:
    arg_keys = jax.random.split(jax.random.key(seed), 6)
    part_splits = jax.random.split(jax.random.fold_in(arg_keys[5], part), 6)
    return {
        "hidden": bell_draw(part_splits[0], (EXPERTS, ROWS, FF), 0.3, 1.75, ((0, 4), (2, 4))),
        "w_down": heavy_noise(arg_keys[1], (EXPERTS, FF, D), FF ** -0.5, 0.09375, ((0, 4), (1, 4)), (1, 2, 4, 2.0)),
        "upstream": bell_draw(part_splits[2], (TOKENS, D), 1.0, 6.0, ((0, 4), (1, 4))),
        "expert_ids": draw_expert_ids(jax.random.fold_in(jax.random.fold_in(arg_keys[5], part), 71), part),
        "combine": draw_combine(jax.random.fold_in(jax.random.fold_in(arg_keys[5], part), 71), part),
    }


def slot_numbers(expert_ids):
    blocks = expert_ids.reshape(N_EP, TOK_DEV * TOP)
    table = (blocks[:, :, None] == jnp.arange(EXPERTS, dtype=jnp.int32)[None, None, :]).astype(jnp.int32)
    running = jnp.cumsum(table, axis=1, dtype=jnp.int32) - table
    slot_index = jnp.sum(running * table, axis=2).astype(jnp.int32)
    return slot_index.reshape(TOKENS, TOP)


def expert_forward(pair):
    hidden_one, weight_one = pair
    left = hidden_one.reshape(ROWS, N_ET, FF // N_ET).astype(jnp.float32)
    right = weight_one.reshape(N_ET, FF // N_ET, D).astype(jnp.float32)
    parts = jnp.einsum("rbh,bhd->brd", left, right).astype(jnp.bfloat16)
    parts = lax.optimization_barrier(parts).astype(jnp.float32)
    return jnp.sum(parts, axis=0).astype(jnp.bfloat16)


def expert_backward(triple):
    hidden_one, weight_one, routed_one = triple
    grad_h = jnp.dot(routed_one, weight_one.T, preferred_element_type=jnp.float32).astype(jnp.bfloat16)
    grad_w = jnp.dot(hidden_one.T, routed_one, preferred_element_type=jnp.float32).astype(jnp.bfloat16)
    return grad_h, grad_w


def reference(hidden, w_down, upstream, expert_ids, combine):
    slot_index = slot_numbers(expert_ids)
    block_of = (jnp.arange(TOKENS, dtype=jnp.int32) // TOK_DEV).astype(jnp.int32)
    row_index = block_of[:, None] * CAP + slot_index
    flat_index = (expert_ids * ROWS + row_index).reshape(-1).astype(jnp.int32)
    expert_out = lax.map(expert_forward, (hidden, w_down))
    picked = jnp.take(expert_out.reshape(EXPERTS * ROWS, D), flat_index, axis=0)
    picked = picked.astype(jnp.float32).reshape(TOKENS, TOP, D)
    mixed = jnp.sum(picked * combine[:, :, None], axis=1).astype(jnp.bfloat16)
    scaled = (combine[:, :, None] * upstream[:, None, :].astype(jnp.float32)).astype(jnp.bfloat16)
    routed = jnp.zeros((EXPERTS * ROWS, D), jnp.bfloat16).at[flat_index].set(scaled.reshape(TOKENS * TOP, D))
    routed = routed.reshape(EXPERTS, ROWS, D)
    grad_hidden, grad_weight = lax.map(expert_backward, (hidden, w_down, routed))
    table = (expert_ids.reshape(-1)[:, None] == jnp.arange(EXPERTS, dtype=jnp.int32)[None, :]).astype(jnp.float32)
    counts = jnp.sum(table, axis=0)
    masses = jnp.sum(table * combine.reshape(-1)[:, None], axis=0)
    balance = EXPERTS * jnp.sum(counts * masses) / (TOP * TOKENS * TOKENS)
    return mixed, grad_hidden, grad_weight, jnp.reshape(balance, (1,)).astype(jnp.float32)
```

```python
import functools

import jax
import jax.numpy as jnp
from jax import lax
from jax.experimental import pallas as pl
from jax.experimental.pallas import tpu as pltpu
from jax.sharding import PartitionSpec as P

F32 = jnp.float32
BF16 = jnp.bfloat16
VMEM_LIMIT = 40 * 1024 * 1024


def token_table(ids, combine, experts_all):
    tokens = ids.shape[0]
    columns = lax.broadcasted_iota(jnp.int32, (tokens, experts_all), 1)
    named = jnp.zeros((tokens, experts_all), F32)
    weight = jnp.zeros((tokens, experts_all), F32)
    for k in range(ids.shape[1]):
        hit = ids[:, k : k + 1] == columns
        named = named + jnp.where(hit, 1.0, 0.0)
        weight = weight + jnp.where(hit, combine[:, k : k + 1], 0.0)
    rows = lax.broadcasted_iota(jnp.int32, (tokens, tokens), 0)
    cols = lax.broadcasted_iota(jnp.int32, (tokens, tokens), 1)
    earlier = jnp.where(cols < rows, 1.0, 0.0).astype(BF16)
    slot = jnp.dot(earlier, named.astype(BF16), preferred_element_type=F32)
    return named, weight, slot


def pick_column(table, expert):
    columns = lax.broadcasted_iota(jnp.int32, table.shape, 1)
    return jnp.sum(jnp.where(columns == expert, table, 0.0), axis=1, keepdims=True)


def slot_matrix(named, slot, expert, capacity):
    hit = pick_column(named, expert) > 0.5
    place = pick_column(slot, expert).astype(jnp.int32)
    slots = lax.broadcasted_iota(jnp.int32, (named.shape[0], capacity), 1)
    return jnp.where((slots == place) & hit, 1.0, 0.0).astype(BF16)


def route_kernel(experts_all, capacity, me_ref, ids_ref, comb_ref, up_ref, *outs):
    me = me_ref[0]
    named, weight, slot = token_table(ids_ref[...], comb_ref[...], experts_all)
    upstream = up_ref[...].astype(F32)
    for s in range(experts_all):
        expert = lax.rem(me + s, experts_all)
        onehot = slot_matrix(named, slot, expert, capacity)
        scaled = (pick_column(weight, expert) * upstream).astype(BF16)
        outs[s][...] = lax.dot_general(
            onehot, scaled, (((0,), (0,)), ((), ())), preferred_element_type=F32
        ).astype(BF16)
    stats = outs[experts_all]
    stats[...] = jnp.zeros_like(stats)
    stats[0:1, 0:experts_all] = jnp.sum(named, axis=0, keepdims=True)
    stats[1:2, 0:experts_all] = jnp.sum(weight, axis=0, keepdims=True)


def route(me, ids, combine, upstream, experts_all, capacity):
    width = upstream.shape[1]
    vmem = pl.BlockSpec(memory_space=pltpu.VMEM)
    return pl.pallas_call(
        functools.partial(route_kernel, experts_all, capacity),
        out_shape=[jax.ShapeDtypeStruct((capacity, width), BF16)] * experts_all
        + [jax.ShapeDtypeStruct((8, 128), F32)],
        in_specs=[pl.BlockSpec(memory_space=pltpu.SMEM), vmem, vmem, vmem],
        out_specs=[vmem] * (experts_all + 1),
        compiler_params=pltpu.CompilerParams(vmem_limit_bytes=VMEM_LIMIT),
        name="route",
    )(me, ids, combine, upstream)


def mix_kernel(experts_all, capacity, me_ref, ids_ref, comb_ref, *refs):
    me = me_ref[0]
    out_ref = refs[experts_all]
    named, weight, slot = token_table(ids_ref[...], comb_ref[...], experts_all)
    total = None
    for s in range(experts_all):
        expert = lax.rem(me - s + experts_all, experts_all)
        onehot = slot_matrix(named, slot, expert, capacity)
        rows = jnp.dot(onehot, refs[s][...], preferred_element_type=F32)
        term = pick_column(weight, expert) * rows
        total = term if total is None else total + term
    out_ref[...] = total.astype(BF16)


def mix(me, ids, combine, returned, experts_all, capacity):
    width = returned[0].shape[1]
    vmem = pl.BlockSpec(memory_space=pltpu.VMEM)
    return pl.pallas_call(
        functools.partial(mix_kernel, experts_all, capacity),
        out_shape=jax.ShapeDtypeStruct((ids.shape[0], width), BF16),
        in_specs=[pl.BlockSpec(memory_space=pltpu.SMEM)] + [vmem] * (2 + experts_all),
        out_specs=vmem,
        compiler_params=pltpu.CompilerParams(vmem_limit_bytes=VMEM_LIMIT),
        name="mix",
    )(me, ids, combine, *returned)


def cost(rows, depth, columns):
    return pl.CostEstimate(
        flops=2 * rows * depth * columns,
        bytes_accessed=2 * (rows * depth + depth * columns + rows * columns),
        transcendentals=0,
    )


def tile_of(size, most):
    tile = min(size, most)
    while size % tile:
        tile //= 2
    return tile


def forward_kernel(j_ref, hidden_ref, w_ref, *refs):
    total = jnp.dot(hidden_ref[...], w_ref[...], preferred_element_type=F32)
    for extra in refs[:-1]:
        total = total + extra[...].astype(F32)
    refs[-1][...] = total.astype(BF16)


def forward_block(block, hidden, weight, width, extras=()):
    rows, depth = hidden.shape
    tile = tile_of(width, 256)
    tiles = width // tile
    out_spec = pl.BlockSpec((rows, tile), lambda i, j: (0, i))
    return pl.pallas_call(
        forward_kernel,
        out_shape=jax.ShapeDtypeStruct((rows, width), BF16),
        grid_spec=pltpu.PrefetchScalarGridSpec(
            num_scalar_prefetch=1,
            grid=(tiles,),
            in_specs=[
                pl.BlockSpec((rows, depth), lambda i, j: (0, 0)),
                pl.BlockSpec((depth, tile), lambda i, j: (0, j[0] * tiles + i)),
            ]
            + [out_spec] * len(extras),
            out_specs=out_spec,
        ),
        cost_estimate=cost(rows, depth, width),
        compiler_params=pltpu.CompilerParams(vmem_limit_bytes=VMEM_LIMIT),
        name="forward",
    )(block, hidden, weight, *extras)


def grad_h_kernel(blocks, width, j_ref, w_ref, *refs):
    total = None
    for q in range(blocks):
        start = pl.multiple_of(j_ref[q] * width, width)
        term = lax.dot_general(
            refs[q][...],
            w_ref[:, pl.ds(start, width)],
            (((1,), (1,)), ((), ())),
            preferred_element_type=F32,
        )
        total = term if total is None else total + term
    refs[blocks][...] = total.astype(BF16)


def grad_hidden_of(order, weight, pieces):
    depth, model = weight.shape
    rows, width = pieces[0].shape
    blocks = len(pieces)
    tile = tile_of(depth, 256)
    return pl.pallas_call(
        functools.partial(grad_h_kernel, blocks, width),
        out_shape=jax.ShapeDtypeStruct((rows, depth), BF16),
        grid_spec=pltpu.PrefetchScalarGridSpec(
            num_scalar_prefetch=1,
            grid=(depth // tile,),
            in_specs=[pl.BlockSpec((tile, model), lambda i, j: (i, 0))]
            + [pl.BlockSpec((rows, width), lambda i, j: (0, 0))] * blocks,
            out_specs=pl.BlockSpec((rows, tile), lambda i, j: (0, i)),
        ),
        cost_estimate=cost(rows, model, depth),
        compiler_params=pltpu.CompilerParams(vmem_limit_bytes=VMEM_LIMIT),
        name="grad_hidden",
    )(order, weight, *pieces)


def grad_w_kernel(has_base, j_ref, hidden_ref, piece_ref, *refs):
    refs[-1][...] = lax.dot_general(
        hidden_ref[...], piece_ref[...], (((0,), (0,)), ((), ())), preferred_element_type=F32
    ).astype(BF16)


def grad_weight_block(block, hidden, piece, model, base=None):
    rows, depth = hidden.shape
    width = piece.shape[1]
    tile = tile_of(depth, 512)
    extra = [] if base is None else [base]
    return pl.pallas_call(
        functools.partial(grad_w_kernel, bool(extra)),
        out_shape=jax.ShapeDtypeStruct((depth, model), BF16),
        grid_spec=pltpu.PrefetchScalarGridSpec(
            num_scalar_prefetch=1,
            grid=(depth // tile,),
            in_specs=[
                pl.BlockSpec((rows, tile), lambda i, j: (0, i)),
                pl.BlockSpec((rows, width), lambda i, j: (0, 0)),
            ]
            + [pl.BlockSpec(memory_space=pl.ANY)] * len(extra),
            out_specs=pl.BlockSpec((tile, width), lambda i, j: (i, j[0])),
        ),
        input_output_aliases={3: 0} if extra else {},
        cost_estimate=cost(depth, rows, width),
        compiler_params=pltpu.CompilerParams(vmem_limit_bytes=VMEM_LIMIT),
        name="grad_weight",
    )(block, hidden, piece, *extra)


def on_device(hidden, w_down, upstream, expert_ids, combine):
    experts_all = lax.axis_size("ep")
    et = lax.axis_size("et")
    chips = et // 2
    me = lax.axis_index("ep").astype(jnp.int32)
    here = lax.axis_index("et").astype(jnp.int32)
    tokens_here = upstream.shape[0]
    top_count = combine.shape[1]
    hidden_local = hidden[0]
    weight_local = w_down[0]
    capacity = hidden_local.shape[0] // experts_all
    model = weight_local.shape[1]
    width = model // et
    me_ref = me.reshape(1)

    def to_expert(x, s):
        return lax.ppermute(x, "ep", [(i, (i + s) % experts_all) for i in range(experts_all)])

    def to_core(x):
        return lax.ppermute(x, "et", [(i, i ^ 1) for i in range(et)])

    def to_chip(x, d):
        return lax.ppermute(x, "et", [(i, (i + 2 * d) % et) for i in range(et)])

    *routed, stats = route(me_ref, expert_ids, combine, upstream, experts_all, capacity)
    arrived = [routed[0]] + [to_expert(routed[s], s) for s in range(1, experts_all)]
    all_stats = [stats] + [to_expert(stats, s) for s in range(1, experts_all)]

    core_sums = []
    for d in list(range(1, chips)) + [0]:
        mine = lax.rem(here + 2 * d, et)
        other = mine + 1 - 2 * lax.rem(mine, 2)
        sent = to_core(forward_block(other.reshape(1), hidden_local, weight_local, width))
        block = forward_block(mine.reshape(1), hidden_local, weight_local, width, () if d else (sent,))
        if d:
            block = (block.astype(F32) + sent.astype(F32)).astype(BF16)
        core_sums.append(to_chip(block, d) if d else block)

    def result_rows(s):
        start = lax.rem(me + s, experts_all) * capacity
        parts = [lax.dynamic_slice_in_dim(x, start, capacity, 0).astype(F32) for x in core_sums]
        return functools.reduce(jnp.add, parts).astype(BF16)

    returned = [result_rows(0)] + [to_expert(result_rows(s), s) for s in range(1, experts_all)]
    mixed = mix(me_ref, expert_ids, combine, returned, experts_all, capacity)

    piece = jnp.zeros((experts_all * capacity, width), BF16)
    for s in range(experts_all):
        start = lax.rem(me - s + experts_all, experts_all) * capacity
        piece = lax.dynamic_update_slice_in_dim(piece, arrived[s], start, 0)
    pieces, order = [], []
    for d in range(chips):
        source = lax.rem(here - 2 * d + et, et)
        near = to_chip(piece, d) if d else piece
        pieces += [near, to_core(near)]
        order += [source, source + 1 - 2 * lax.rem(source, 2)]
    grad_w = None
    for block, near in zip(order, pieces):
        grad_w = grad_weight_block(block.reshape(1), hidden_local, near, model, grad_w)
    grad_h = grad_hidden_of(jnp.stack(order), weight_local, pieces)

    table = sum(
        jnp.where(
            (lax.rem(me - s + experts_all, experts_all) == jnp.arange(experts_all))[:, None, None],
            all_stats[s][None, :2, :experts_all],
            0.0,
        )
        for s in range(experts_all)
    )
    totals = jnp.sum(table, axis=0)
    tokens_all = tokens_here * experts_all
    balance = experts_all * jnp.sum(totals[0] * totals[1]) / (top_count * tokens_all * tokens_all)
    return (mixed, grad_h[None], grad_w[None], jnp.reshape(balance, (1,)))


def solution(mesh):
    placed = (
        P(("groups", "ep"), None, "et"),
        P("ep", "et", None),
        P(("groups", "ep"), "et"),
        P(("groups", "ep"), None),
        P(("groups", "ep"), None),
    )
    return jax.shard_map(
        on_device,
        mesh=mesh,
        in_specs=placed,
        out_specs=(
            P(("groups", "ep"), "et"),
            P(("groups", "ep"), None, "et"),
            P(("groups", "ep"), "et", None),
            P("groups"),
        ),
        check_vma=False,
    )
```

```python
import functools

import jax
import jax.numpy as jnp
from jax import lax
from jax.experimental import pallas as pl
from jax.experimental.pallas import tpu as pltpu
from jax.sharding import PartitionSpec as P

F32 = jnp.float32
BF16 = jnp.bfloat16
VMEM_LIMIT = 50 * 1024 * 1024


def token_table(ids, combine, experts_all):
    tokens = ids.shape[0]
    columns = lax.broadcasted_iota(jnp.int32, (tokens, experts_all), 1)
    named = jnp.zeros((tokens, experts_all), F32)
    weight = jnp.zeros((tokens, experts_all), F32)
    for k in range(ids.shape[1]):
        hit = ids[:, k : k + 1] == columns
        named = named + jnp.where(hit, 1.0, 0.0)
        weight = weight + jnp.where(hit, combine[:, k : k + 1], 0.0)
    rows = lax.broadcasted_iota(jnp.int32, (tokens, tokens), 0)
    cols = lax.broadcasted_iota(jnp.int32, (tokens, tokens), 1)
    earlier = jnp.where(cols < rows, 1.0, 0.0).astype(BF16)
    slot = jnp.dot(earlier, named.astype(BF16), preferred_element_type=F32)
    return named, weight, slot


def pick_column(table, expert):
    columns = lax.broadcasted_iota(jnp.int32, table.shape, 1)
    return jnp.sum(jnp.where(columns == expert, table, 0.0), axis=1, keepdims=True)


def slot_matrix(named, slot, expert, capacity):
    hit = pick_column(named, expert) > 0.5
    place = pick_column(slot, expert).astype(jnp.int32)
    slots = lax.broadcasted_iota(jnp.int32, (named.shape[0], capacity), 1)
    return jnp.where((slots == place) & hit, 1.0, 0.0).astype(BF16)


def route_kernel(experts_all, capacity, me_ref, ids_ref, comb_ref, up_ref, *outs):
    me = me_ref[0]
    named, weight, slot = token_table(ids_ref[...], comb_ref[...], experts_all)
    upstream = up_ref[...].astype(F32)
    for s in range(experts_all):
        expert = lax.rem(me + s, experts_all)
        onehot = slot_matrix(named, slot, expert, capacity)
        scaled = (pick_column(weight, expert) * upstream).astype(BF16)
        outs[s][...] = lax.dot_general(
            onehot, scaled, (((0,), (0,)), ((), ())), preferred_element_type=F32
        ).astype(BF16)
    stats = outs[experts_all]
    stats[...] = jnp.zeros_like(stats)
    stats[0:1, 0:experts_all] = jnp.sum(named, axis=0, keepdims=True)
    stats[1:2, 0:experts_all] = jnp.sum(weight, axis=0, keepdims=True)


def route(me, ids, combine, upstream, experts_all, capacity):
    width = upstream.shape[1]
    vmem = pl.BlockSpec(memory_space=pltpu.VMEM)
    return pl.pallas_call(
        functools.partial(route_kernel, experts_all, capacity),
        out_shape=[jax.ShapeDtypeStruct((capacity, width), BF16)] * experts_all
        + [jax.ShapeDtypeStruct((8, 128), F32)],
        in_specs=[pl.BlockSpec(memory_space=pltpu.SMEM), vmem, vmem, vmem],
        out_specs=[vmem] * (experts_all + 1),
        compiler_params=pltpu.CompilerParams(vmem_limit_bytes=VMEM_LIMIT),
        name="route",
    )(me, ids, combine, upstream)


def mix_kernel(experts_all, capacity, me_ref, ids_ref, comb_ref, *refs):
    me = me_ref[0]
    out_ref = refs[experts_all]
    named, weight, slot = token_table(ids_ref[...], comb_ref[...], experts_all)
    total = None
    for s in range(experts_all):
        expert = lax.rem(me - s + experts_all, experts_all)
        onehot = slot_matrix(named, slot, expert, capacity)
        rows = jnp.dot(onehot, refs[s][...], preferred_element_type=F32)
        term = pick_column(weight, expert) * rows
        total = term if total is None else total + term
    out_ref[...] = total.astype(BF16)


def mix(me, ids, combine, returned, experts_all, capacity):
    width = returned[0].shape[1]
    vmem = pl.BlockSpec(memory_space=pltpu.VMEM)
    return pl.pallas_call(
        functools.partial(mix_kernel, experts_all, capacity),
        out_shape=jax.ShapeDtypeStruct((ids.shape[0], width), BF16),
        in_specs=[pl.BlockSpec(memory_space=pltpu.SMEM)] + [vmem] * (2 + experts_all),
        out_specs=vmem,
        compiler_params=pltpu.CompilerParams(vmem_limit_bytes=VMEM_LIMIT),
        name="mix",
    )(me, ids, combine, *returned)


def cost(rows, depth, columns):
    return pl.CostEstimate(
        flops=2 * rows * depth * columns,
        bytes_accessed=2 * (rows * depth + depth * columns + rows * columns),
        transcendentals=0,
    )


def tile_of(size, most):
    tile = min(size, most)
    while size % tile:
        tile //= 2
    return tile


def forward_kernel(extras, j_ref, hidden_ref, w_ref, *refs):
    total = jnp.dot(hidden_ref[...], w_ref[...], preferred_element_type=F32)
    for extra in refs[:extras]:
        total = total + extra[...].astype(F32)
    refs[-1][...] = total.astype(BF16)


def forward_block(block, hidden, weight, width, extras=(), after=()):
    rows, depth = hidden.shape
    tile = tile_of(width, 512)
    tiles = width // tile
    out_spec = pl.BlockSpec((rows, tile), lambda i, j: (0, i))
    return pl.pallas_call(
        functools.partial(forward_kernel, len(extras)),
        out_shape=jax.ShapeDtypeStruct((rows, width), BF16),
        grid_spec=pltpu.PrefetchScalarGridSpec(
            num_scalar_prefetch=1,
            grid=(tiles,),
            in_specs=[
                pl.BlockSpec((rows, depth), lambda i, j: (0, 0)),
                pl.BlockSpec((depth, tile), lambda i, j: (0, j[0] * tiles + i)),
            ]
            + [out_spec] * len(extras)
            + [pl.BlockSpec(memory_space=pl.ANY)] * len(after),
            out_specs=out_spec,
        ),
        cost_estimate=cost(rows, depth, width),
        compiler_params=pltpu.CompilerParams(vmem_limit_bytes=VMEM_LIMIT),
        name="forward",
    )(block, hidden, weight, *extras, *after)


def last_forward_kernel(extras, experts_all, capacity, j_ref, hidden_ref, w_ref, *refs):
    outs, scratch = refs[extras + 1 : -1], refs[-1]
    total = jnp.dot(hidden_ref[...], w_ref[...], preferred_element_type=F32)
    for extra in refs[:extras]:
        total = total + extra[...].astype(F32)
    scratch[...] = total.astype(BF16)
    for s in range(experts_all):
        start = pl.multiple_of(lax.rem(j_ref[1] + s, experts_all) * capacity, capacity)
        outs[s][...] = scratch[pl.ds(start, capacity), :]
    outs[experts_all][...] = refs[extras][...]


def last_forward_block(block, hidden, weight, width, extras, stats, experts_all):
    rows, depth = hidden.shape
    capacity = rows // experts_all
    tile = tile_of(width, 512)
    tiles = width // tile
    stats_spec = pl.BlockSpec(stats.shape, lambda i, j: (0, 0))
    return pl.pallas_call(
        functools.partial(last_forward_kernel, len(extras), experts_all, capacity),
        out_shape=[jax.ShapeDtypeStruct((capacity, width), BF16)] * experts_all
        + [jax.ShapeDtypeStruct(stats.shape, stats.dtype)],
        grid_spec=pltpu.PrefetchScalarGridSpec(
            num_scalar_prefetch=1,
            grid=(tiles,),
            in_specs=[
                pl.BlockSpec((rows, depth), lambda i, j: (0, 0)),
                pl.BlockSpec((depth, tile), lambda i, j: (0, j[0] * tiles + i)),
            ]
            + [pl.BlockSpec((rows, tile), lambda i, j: (0, i))] * len(extras)
            + [stats_spec],
            out_specs=[pl.BlockSpec((capacity, tile), lambda i, j: (0, i))] * experts_all
            + [stats_spec],
            scratch_shapes=[pltpu.VMEM((rows, tile), BF16)],
        ),
        cost_estimate=cost(rows, depth, width),
        compiler_params=pltpu.CompilerParams(vmem_limit_bytes=VMEM_LIMIT),
        name="last_forward",
    )(block, hidden, weight, *extras, stats)


def add_kernel(a_ref, b_ref, out_ref):
    out_ref[...] = (a_ref[...].astype(F32) + b_ref[...].astype(F32)).astype(BF16)


def add(a, b):
    rows, width = a.shape
    spec = pl.BlockSpec((tile_of(rows, 256), width), lambda i: (i, 0))
    return pl.pallas_call(
        add_kernel,
        out_shape=jax.ShapeDtypeStruct(a.shape, BF16),
        grid=(rows // spec.block_shape[0],),
        in_specs=[spec, spec],
        out_specs=spec,
        compiler_params=pltpu.CompilerParams(vmem_limit_bytes=VMEM_LIMIT),
        name="add",
    )(a, b)


def grads_kernel(experts_all, first, last, tile, j_ref, hidden_ref, w_ref, *refs):
    pieces, rest = refs[:4], refs[4:]
    out_w, out_h, scratch = rest[-3:]
    step = pl.program_id(0)
    core, me = j_ref[1], j_ref[2]
    capacity, width = pieces[0].shape

    @pl.when(step == 0)
    def _():
        for half in range(2):
            side = core if half == 0 else 1 - core
            column = pl.multiple_of(side * width, width)
            for s in range(experts_all):
                owner = lax.rem(me - s + experts_all, experts_all)
                row = pl.multiple_of(owner * capacity, capacity)
                if s == 0:
                    rows = pieces[2 * half][...]
                else:
                    rows = pieces[2 * half + 1][(s - 1) * capacity : s * capacity, :]
                scratch[pl.ds(row, capacity), pl.ds(column, width)] = rows

    columns = scratch[:, pl.ds(pl.multiple_of(step * tile, tile), tile)]
    out_w[...] = lax.dot_general(
        hidden_ref[...], columns, (((0,), (0,)), ((), ())), preferred_element_type=F32
    ).astype(BF16)
    total = lax.dot_general(
        scratch[...], w_ref[...], (((1,), (1,)), ((), ())), preferred_element_type=F32
    )
    if not first:
        total = total + rest[0][...]
    out_h[...] = total.astype(out_h.dtype)


def grads(place, hidden, weight, pieces, experts_all, before, last):
    rows, depth = hidden.shape
    model = weight.shape[1]
    width = pieces[0].shape[1]
    chip_width = 2 * width
    steps = max(1, min(chip_width, depth) // 512)
    tile_w, tile_h = chip_width // steps, depth // steps
    whole = lambda x: pl.BlockSpec(x.shape, lambda i, j: (0, 0))
    h_spec = pl.BlockSpec((rows, tile_h), lambda i, j: (0, i))
    first = before is None
    extra = [] if first else [before[1], before[0]]
    return pl.pallas_call(
        functools.partial(grads_kernel, experts_all, first, last, tile_w),
        out_shape=[
            jax.ShapeDtypeStruct((depth, model), BF16),
            jax.ShapeDtypeStruct((rows, depth), BF16 if last else F32),
        ],
        grid_spec=pltpu.PrefetchScalarGridSpec(
            num_scalar_prefetch=1,
            grid=(steps,),
            in_specs=[
                whole(hidden),
                pl.BlockSpec((tile_h, chip_width), lambda i, j: (i, j[0])),
            ]
            + [whole(x) for x in pieces]
            + ([] if first else [h_spec, pl.BlockSpec(memory_space=pl.ANY)]),
            out_specs=[
                pl.BlockSpec((depth, tile_w), lambda i, j: (0, j[0] * steps + i)),
                h_spec,
            ],
            scratch_shapes=[pltpu.VMEM((rows, chip_width), BF16)],
        ),
        input_output_aliases={} if first else {8: 0},
        cost_estimate=cost(rows, depth, 2 * chip_width),
        compiler_params=pltpu.CompilerParams(vmem_limit_bytes=VMEM_LIMIT),
        name="grads",
    )(place, hidden, weight, *pieces, *extra)


def on_device(hidden, w_down, upstream, expert_ids, combine):
    experts_all = lax.axis_size("ep")
    et = lax.axis_size("et")
    chips = et // 2
    me = lax.axis_index("ep").astype(jnp.int32)
    here = lax.axis_index("et").astype(jnp.int32)
    core = lax.rem(here, 2)
    tokens_here = upstream.shape[0]
    top_count = combine.shape[1]
    hidden_local = hidden[0]
    weight_local = w_down[0]
    capacity = hidden_local.shape[0] // experts_all
    model = weight_local.shape[1]
    width = model // et
    me_ref = me.reshape(1)

    def to_expert(x, s):
        return lax.ppermute(x, "ep", [(i, (i + s) % experts_all) for i in range(experts_all)])

    def to_core(x):
        return lax.ppermute(x, "et", [(i, i ^ 1) for i in range(et)])

    def to_chip(x, d):
        return lax.ppermute(x, "et", [(i, (i + 2 * d) % et) for i in range(et)])

    *routed, stats = route(me_ref, expert_ids, combine, upstream, experts_all, capacity)
    own_rows = routed[0]
    own_at = [to_chip(own_rows, d) if d else own_rows for d in range(chips)]
    far_rows = jnp.concatenate([to_expert(routed[s], s) for s in range(1, experts_all)], axis=0)

    arrived, after = [], ()
    for d in range(1, chips):
        mine = lax.rem(here + 2 * d, et)
        other = mine + 1 - 2 * core
        sent = forward_block(other.reshape(1), hidden_local, weight_local, width, (), after)
        block = forward_block(mine.reshape(1), hidden_local, weight_local, width, (), (sent,))
        after = (block,)
        arrived.append(to_chip(add(block, to_core(sent)), d))
    other = here + 1 - 2 * core
    sent = to_core(forward_block(other.reshape(1), hidden_local, weight_local, width, (), after))

    far_at = [to_chip(far_rows, d) if d else far_rows for d in range(chips)]
    gradients = None
    results = None
    for d in range(chips):
        chip = lax.rem(here // 2 - d + chips, chips)
        pieces = [own_at[d], far_at[d], to_core(own_at[d]), to_core(far_at[d])]
        place = jnp.stack([chip, core, me])
        gradients = grads(
            place, hidden_local, weight_local, pieces, experts_all, gradients, d == chips - 1
        )
        if d == 0:
            results = last_forward_block(
                jnp.stack([here, me]), hidden_local, weight_local, width, [sent, *arrived], stats, experts_all
            )
    grad_w, grad_h = gradients

    *result, stats_late = results
    returned = [result[0]] + [to_expert(result[s], s) for s in range(1, experts_all)]
    all_stats = [stats_late] + [to_expert(stats_late, s) for s in range(1, experts_all)]
    mixed = mix(me_ref, expert_ids, combine, returned, experts_all, capacity)

    table = sum(
        jnp.where(
            (lax.rem(me - s + experts_all, experts_all) == jnp.arange(experts_all))[:, None, None],
            all_stats[s][None, :2, :experts_all],
            0.0,
        )
        for s in range(experts_all)
    )
    totals = jnp.sum(table, axis=0)
    tokens_all = tokens_here * experts_all
    balance = experts_all * jnp.sum(totals[0] * totals[1]) / (top_count * tokens_all * tokens_all)
    return (mixed, grad_h[None], grad_w[None], jnp.reshape(balance, (1,)))


def solution(mesh):
    placed = (
        P(("groups", "ep"), None, "et"),
        P("ep", "et", None),
        P(("groups", "ep"), "et"),
        P(("groups", "ep"), None),
        P(("groups", "ep"), None),
    )
    return jax.shard_map(
        on_device,
        mesh=mesh,
        in_specs=placed,
        out_specs=(
            P(("groups", "ep"), "et"),
            P(("groups", "ep"), None, "et"),
            P(("groups", "ep"), "et", None),
            P("groups"),
        ),
        check_vma=False,
    )
```

```python
import functools

import jax
import jax.numpy as jnp
from jax import lax
from jax.experimental import pallas as pl
from jax.experimental.pallas import tpu as pltpu
from jax.sharding import PartitionSpec as P

F32 = jnp.float32
BF16 = jnp.bfloat16
VMEM_LIMIT = 50 * 1024 * 1024


def token_table(ids, combine, experts_all):
    tokens = ids.shape[0]
    columns = lax.broadcasted_iota(jnp.int32, (tokens, experts_all), 1)
    named = jnp.zeros((tokens, experts_all), F32)
    weight = jnp.zeros((tokens, experts_all), F32)
    for k in range(ids.shape[1]):
        hit = ids[:, k : k + 1] == columns
        named = named + jnp.where(hit, 1.0, 0.0)
        weight = weight + jnp.where(hit, combine[:, k : k + 1], 0.0)
    rows = lax.broadcasted_iota(jnp.int32, (tokens, tokens), 0)
    cols = lax.broadcasted_iota(jnp.int32, (tokens, tokens), 1)
    earlier = jnp.where(cols < rows, 1.0, 0.0).astype(BF16)
    slot = jnp.dot(earlier, named.astype(BF16), preferred_element_type=F32)
    return named, weight, slot


def pick_column(table, expert):
    columns = lax.broadcasted_iota(jnp.int32, table.shape, 1)
    return jnp.sum(jnp.where(columns == expert, table, 0.0), axis=1, keepdims=True)


def slot_matrix(named, slot, expert, capacity):
    hit = pick_column(named, expert) > 0.5
    place = pick_column(slot, expert).astype(jnp.int32)
    slots = lax.broadcasted_iota(jnp.int32, (named.shape[0], capacity), 1)
    return jnp.where((slots == place) & hit, 1.0, 0.0).astype(BF16)


def route_kernel(experts_all, capacity, me_ref, ids_ref, comb_ref, up_ref, *outs):
    me = me_ref[0]
    named, weight, slot = token_table(ids_ref[...], comb_ref[...], experts_all)
    upstream = up_ref[...].astype(F32)
    for s in range(experts_all):
        expert = lax.rem(me + s, experts_all)
        onehot = slot_matrix(named, slot, expert, capacity)
        scaled = (pick_column(weight, expert) * upstream).astype(BF16)
        outs[s][...] = lax.dot_general(
            onehot, scaled, (((0,), (0,)), ((), ())), preferred_element_type=F32
        ).astype(BF16)
    stats = outs[experts_all]
    stats[...] = jnp.zeros_like(stats)
    stats[0:1, 0:experts_all] = jnp.sum(named, axis=0, keepdims=True)
    stats[1:2, 0:experts_all] = jnp.sum(weight, axis=0, keepdims=True)


def route(me, ids, combine, upstream, experts_all, capacity):
    width = upstream.shape[1]
    vmem = pl.BlockSpec(memory_space=pltpu.VMEM)
    return pl.pallas_call(
        functools.partial(route_kernel, experts_all, capacity),
        out_shape=[jax.ShapeDtypeStruct((capacity, width), BF16)] * experts_all
        + [jax.ShapeDtypeStruct((8, 128), F32)],
        in_specs=[pl.BlockSpec(memory_space=pltpu.SMEM), vmem, vmem, vmem],
        out_specs=[vmem] * (experts_all + 1),
        compiler_params=pltpu.CompilerParams(vmem_limit_bytes=VMEM_LIMIT),
        name="route",
    )(me, ids, combine, upstream)


def mix_kernel(experts_all, capacity, me_ref, ids_ref, comb_ref, *refs):
    me = me_ref[0]
    out_ref = refs[-1]
    named, weight, slot = token_table(ids_ref[...], comb_ref[...], experts_all)
    total = None
    for s in range(experts_all):
        expert = lax.rem(me - s + experts_all, experts_all)
        onehot = slot_matrix(named, slot, expert, capacity)
        rows = jnp.dot(onehot, refs[s][...], preferred_element_type=F32)
        term = pick_column(weight, expert) * rows
        total = term if total is None else total + term
    out_ref[...] = total.astype(BF16)


def mix(me, ids, combine, returned, experts_all, capacity, after=()):
    width = returned[0].shape[1]
    vmem = pl.BlockSpec(memory_space=pltpu.VMEM)
    return pl.pallas_call(
        functools.partial(mix_kernel, experts_all, capacity),
        out_shape=jax.ShapeDtypeStruct((ids.shape[0], width), BF16),
        in_specs=[pl.BlockSpec(memory_space=pltpu.SMEM)] + [vmem] * (2 + experts_all)
        + [pl.BlockSpec(memory_space=pl.ANY)] * len(after),
        out_specs=vmem,
        compiler_params=pltpu.CompilerParams(vmem_limit_bytes=VMEM_LIMIT),
        name="mix",
    )(me, ids, combine, *returned, *after)


def cost(rows, depth, columns):
    return pl.CostEstimate(
        flops=2 * rows * depth * columns,
        bytes_accessed=2 * (rows * depth + depth * columns + rows * columns),
        transcendentals=0,
    )


def tile_of(size, most):
    tile = min(size, most)
    while size % tile:
        tile //= 2
    return tile


def forward_kernel(extras, j_ref, hidden_ref, w_ref, *refs):
    total = jnp.dot(hidden_ref[...], w_ref[...], preferred_element_type=F32)
    for extra in refs[:extras]:
        total = total + extra[...].astype(F32)
    refs[-1][...] = total.astype(BF16)


def forward_block(block, hidden, weight, width, extras=(), after=()):
    rows, depth = hidden.shape
    tile = tile_of(width, 512)
    tiles = width // tile
    out_spec = pl.BlockSpec((rows, tile), lambda i, j: (0, i))
    return pl.pallas_call(
        functools.partial(forward_kernel, len(extras)),
        out_shape=jax.ShapeDtypeStruct((rows, width), BF16),
        grid_spec=pltpu.PrefetchScalarGridSpec(
            num_scalar_prefetch=1,
            grid=(tiles,),
            in_specs=[
                pl.BlockSpec((rows, depth), lambda i, j: (0, 0)),
                pl.BlockSpec((depth, tile), lambda i, j: (0, j[0] * tiles + i)),
            ]
            + [out_spec] * len(extras)
            + [pl.BlockSpec(memory_space=pl.ANY)] * len(after),
            out_specs=out_spec,
        ),
        cost_estimate=cost(rows, depth, width),
        compiler_params=pltpu.CompilerParams(vmem_limit_bytes=VMEM_LIMIT),
        name="forward",
    )(block, hidden, weight, *extras, *after)


def last_forward_kernel(extras, experts_all, capacity, j_ref, hidden_ref, w_ref, *refs):
    outs, scratch = refs[-experts_all - 2 : -1], refs[-1]
    total = jnp.dot(hidden_ref[...], w_ref[...], preferred_element_type=F32)
    for extra in refs[:extras]:
        total = total + extra[...].astype(F32)
    scratch[...] = total.astype(BF16)
    for s in range(experts_all):
        start = pl.multiple_of(lax.rem(j_ref[1] + s, experts_all) * capacity, capacity)
        outs[s][...] = scratch[pl.ds(start, capacity), :]
    outs[experts_all][...] = refs[extras][...]


def last_forward_block(block, hidden, weight, width, extras, stats, experts_all, after=()):
    rows, depth = hidden.shape
    capacity = rows // experts_all
    tile = tile_of(width, 512)
    tiles = width // tile
    stats_spec = pl.BlockSpec(stats.shape, lambda i, j: (0, 0))
    return pl.pallas_call(
        functools.partial(last_forward_kernel, len(extras), experts_all, capacity),
        out_shape=[jax.ShapeDtypeStruct((capacity, width), BF16)] * experts_all
        + [jax.ShapeDtypeStruct(stats.shape, stats.dtype)],
        grid_spec=pltpu.PrefetchScalarGridSpec(
            num_scalar_prefetch=1,
            grid=(tiles,),
            in_specs=[
                pl.BlockSpec((rows, depth), lambda i, j: (0, 0)),
                pl.BlockSpec((depth, tile), lambda i, j: (0, j[0] * tiles + i)),
            ]
            + [pl.BlockSpec((rows, tile), lambda i, j: (0, i))] * len(extras)
            + [stats_spec]
            + [pl.BlockSpec(memory_space=pl.ANY)] * len(after),
            out_specs=[pl.BlockSpec((capacity, tile), lambda i, j: (0, i))] * experts_all
            + [stats_spec],
            scratch_shapes=[pltpu.VMEM((rows, tile), BF16)],
        ),
        cost_estimate=cost(rows, depth, width),
        compiler_params=pltpu.CompilerParams(vmem_limit_bytes=VMEM_LIMIT),
        name="last_forward",
    )(block, hidden, weight, *extras, stats, *after)


def join_kernel(parts, *refs):
    capacity = refs[0].shape[0]
    for n in range(parts):
        refs[-1][n * capacity : (n + 1) * capacity, :] = refs[n][...]


def join(parts, after):
    capacity, width = parts[0].shape
    vmem = pl.BlockSpec(memory_space=pltpu.VMEM)
    return pl.pallas_call(
        functools.partial(join_kernel, len(parts)),
        out_shape=jax.ShapeDtypeStruct((len(parts) * capacity, width), BF16),
        in_specs=[vmem] * len(parts) + [pl.BlockSpec(memory_space=pl.ANY)],
        out_specs=vmem,
        name="join",
    )(*parts, after)


def hold_kernel(*refs):
    pass


def hold(x, after):
    anywhere = pl.BlockSpec(memory_space=pl.ANY)
    return pl.pallas_call(
        hold_kernel,
        out_shape=jax.ShapeDtypeStruct(x.shape, x.dtype),
        in_specs=[anywhere, anywhere],
        out_specs=anywhere,
        input_output_aliases={0: 0},
        name="hold",
    )(x, after)


def add_kernel(a_ref, b_ref, out_ref):
    out_ref[...] = (a_ref[...].astype(F32) + b_ref[...].astype(F32)).astype(BF16)


def add(a, b):
    rows, width = a.shape
    spec = pl.BlockSpec((tile_of(rows, 256), width), lambda i: (i, 0))
    return pl.pallas_call(
        add_kernel,
        out_shape=jax.ShapeDtypeStruct(a.shape, BF16),
        grid=(rows // spec.block_shape[0],),
        in_specs=[spec, spec],
        out_specs=spec,
        compiler_params=pltpu.CompilerParams(vmem_limit_bytes=VMEM_LIMIT),
        name="add",
    )(a, b)


def grads_kernel(experts_all, first, last, tile, j_ref, hidden_ref, w_ref, *refs):
    pieces, rest = refs[:4], refs[4:]
    out_w, out_h, scratch = rest[-3:]
    step = pl.program_id(0)
    core, me = j_ref[1], j_ref[2]
    capacity, width = pieces[0].shape

    @pl.when(step == 0)
    def _():
        for half in range(2):
            side = core if half == 0 else 1 - core
            column = pl.multiple_of(side * width, width)
            for s in range(experts_all):
                owner = lax.rem(me - s + experts_all, experts_all)
                row = pl.multiple_of(owner * capacity, capacity)
                if s == 0:
                    rows = pieces[2 * half][...]
                else:
                    rows = pieces[2 * half + 1][(s - 1) * capacity : s * capacity, :]
                scratch[pl.ds(row, capacity), pl.ds(column, width)] = rows

    columns = scratch[:, pl.ds(pl.multiple_of(step * tile, tile), tile)]
    out_w[...] = lax.dot_general(
        hidden_ref[...], columns, (((0,), (0,)), ((), ())), preferred_element_type=F32
    ).astype(BF16)
    total = lax.dot_general(
        scratch[...], w_ref[...], (((1,), (1,)), ((), ())), preferred_element_type=F32
    )
    if not first:
        total = total + rest[0][...]
    out_h[...] = total.astype(out_h.dtype)


def grads(place, hidden, weight, pieces, experts_all, before, last, after=()):
    rows, depth = hidden.shape
    model = weight.shape[1]
    width = pieces[0].shape[1]
    chip_width = 2 * width
    steps = max(1, min(chip_width, depth) // 512)
    tile_w, tile_h = chip_width // steps, depth // steps
    whole = lambda x: pl.BlockSpec(x.shape, lambda i, j: (0, 0))
    h_spec = pl.BlockSpec((rows, tile_h), lambda i, j: (0, i))
    first = before is None
    extra = [] if first else [before[1], before[0]]
    return pl.pallas_call(
        functools.partial(grads_kernel, experts_all, first, last, tile_w),
        out_shape=[
            jax.ShapeDtypeStruct((depth, model), BF16),
            jax.ShapeDtypeStruct((rows, depth), BF16 if last else F32),
        ],
        grid_spec=pltpu.PrefetchScalarGridSpec(
            num_scalar_prefetch=1,
            grid=(steps,),
            in_specs=[
                whole(hidden),
                pl.BlockSpec((tile_h, chip_width), lambda i, j: (i, j[0])),
            ]
            + [whole(x) for x in pieces]
            + ([] if first else [h_spec, pl.BlockSpec(memory_space=pl.ANY)])
            + [pl.BlockSpec(memory_space=pl.ANY)] * len(after),
            out_specs=[
                pl.BlockSpec((depth, tile_w), lambda i, j: (0, j[0] * steps + i)),
                h_spec,
            ],
            scratch_shapes=[pltpu.VMEM((rows, chip_width), BF16)],
        ),
        input_output_aliases={} if first else {8: 0},
        cost_estimate=cost(rows, depth, 2 * chip_width),
        compiler_params=pltpu.CompilerParams(vmem_limit_bytes=VMEM_LIMIT),
        name="grads",
    )(place, hidden, weight, *pieces, *extra, *after)


def on_device(hidden, w_down, upstream, expert_ids, combine):
    experts_all = lax.axis_size("ep")
    et = lax.axis_size("et")
    chips = et // 2
    me = lax.axis_index("ep").astype(jnp.int32)
    here = lax.axis_index("et").astype(jnp.int32)
    core = lax.rem(here, 2)
    tokens_here = upstream.shape[0]
    top_count = combine.shape[1]
    hidden_local = hidden[0]
    weight_local = w_down[0]
    capacity = hidden_local.shape[0] // experts_all
    model = weight_local.shape[1]
    width = model // et
    me_ref = me.reshape(1)

    def to_expert(x, s):
        return lax.ppermute(x, "ep", [(i, (i + s) % experts_all) for i in range(experts_all)])

    def to_core(x):
        return lax.ppermute(x, "et", [(i, i ^ 1) for i in range(et)])

    def to_chip(x, d):
        return lax.ppermute(x, "et", [(i, (i + 2 * d) % et) for i in range(et)])

    *routed, stats = route(me_ref, expert_ids, combine, upstream, experts_all, capacity)
    own_rows = routed[0]
    own_at = [to_chip(own_rows, d) if d else own_rows for d in range(chips)]
    far_parts = [to_expert(routed[s], s) for s in range(1, experts_all)]

    arrived, after = [], (stats,)
    for d in range(1, chips):
        mine = lax.rem(here + 2 * d, et)
        other = mine + 1 - 2 * core
        sent = forward_block(other.reshape(1), hidden_local, weight_local, width, (), after)
        block = forward_block(mine.reshape(1), hidden_local, weight_local, width, (), (sent,))
        summed = add(block, to_core(sent))
        after = (summed, own_at[d])
        arrived.append(to_chip(summed, d))
    other = here + 1 - 2 * core
    block = forward_block(other.reshape(1), hidden_local, weight_local, width, (), after)
    sent = to_core(block)
    far_rows = join(far_parts, block)

    far_at = [to_chip(far_rows, d) if d else far_rows for d in range(chips)]
    gradients, results, after = None, None, ()
    for d in range(chips):
        chip = lax.rem(here // 2 - d + chips, chips)
        far = hold(far_at[d], gradients[1] if d > 1 else results[-1]) if d else far_at[d]
        pieces = [own_at[d], far, to_core(own_at[d]), to_core(far)]
        place = jnp.stack([chip, core, me])
        gradients = grads(
            place, hidden_local, weight_local, pieces, experts_all, gradients, d == chips - 1, after
        )
        if d == 0:
            results = last_forward_block(
                jnp.stack([here, me]), hidden_local, weight_local, width, [sent, *arrived], stats, experts_all,
                (gradients[1],),
            )
            after = (results[-1],)
    grad_w, grad_h = gradients

    *result, stats_late = results
    returned = [result[0]] + [to_expert(result[s], s) for s in range(1, experts_all)]
    all_stats = [stats_late] + [to_expert(stats_late, s) for s in range(1, experts_all)]
    mixed = mix(me_ref, expert_ids, combine, returned, experts_all, capacity, (grad_h,))

    table = sum(
        jnp.where(
            (lax.rem(me - s + experts_all, experts_all) == jnp.arange(experts_all))[:, None, None],
            all_stats[s][None, :2, :experts_all],
            0.0,
        )
        for s in range(experts_all)
    )
    totals = jnp.sum(table, axis=0)
    tokens_all = tokens_here * experts_all
    balance = experts_all * jnp.sum(totals[0] * totals[1]) / (top_count * tokens_all * tokens_all)
    return (mixed, grad_h[None], grad_w[None], jnp.reshape(balance, (1,)))


def solution(mesh):
    placed = (
        P(("groups", "ep"), None, "et"),
        P("ep", "et", None),
        P(("groups", "ep"), "et"),
        P(("groups", "ep"), None),
        P(("groups", "ep"), None),
    )
    return jax.shard_map(
        on_device,
        mesh=mesh,
        in_specs=placed,
        out_specs=(
            P(("groups", "ep"), "et"),
            P(("groups", "ep"), None, "et"),
            P(("groups", "ep"), "et", None),
            P("groups"),
        ),
        check_vma=False,
    )
```
